32 devices in a mesh: polar: 8 (over y, x, core), azimuth: 4 (over z).
Axes of the slice: x: 2, y: 2, z: 4, core: 2. Of those that a mesh axis runs over, the one named last changes fastest.
Arguments:
- grid_input: bfloat16 [720, 276480], P('polar', 'azimuth'), may hold values from -6 to 6
- cotangent: bfloat16 [720, 192, 1440], P('polar', 'azimuth'), may hold values from -6 to 6
- forward_legendre: bfloat16 [720, 256, 256], P(None, 'polar'), may hold values from -0.21875 to 0.21875
- inverse_legendre: bfloat16 [720, 256, 256], P(None, 'polar'), may hold values from -0.375 to 0.375
- filter_weight: bfloat16 [256, 73728], P('polar'), may hold values from -0.3125 to 0.3125
Outputs:
- filtered: bfloat16 [720, 192, 1440], P('polar', 'azimuth')
- grid_grad: bfloat16 [720, 276480], P('polar', 'azimuth')
The draws below stay inside these ranges and needn't reach their ends.
All inputs are finite; a program needn't handle non-finite values.
Results may differ from the reference program's by a relative error of at most 0.02.
Values may be sent and summed in bfloat16 or wider, within the bound.
A program may use at most 256 MiB of HBM per device.

```python
import math
import jax
import jax.numpy as jnp
from jax import lax

LAT = 720
LON = 1440
C = 192
DEGREES = 256
ORDERS = 256
N_POLAR = 8


def level_of(rng, extent, pieces, low, largest):
    def one(position, blocks):
        draws = jax.random.uniform(jax.random.fold_in(jax.random.fold_in(rng, 6), position), (blocks,), jnp.float32, low / len(pieces), largest / len(pieces))
        return jnp.repeat(jnp.exp(draws), extent[position] // blocks).reshape((-1,) + (1,) * (len(extent) - position - 1))

    level = one(*pieces[0])
    for cut in pieces[1:]:
        level = level * one(*cut)
    return level


def normal_values(stream_key, dims, scale, bound, pieces=(), held_as=jnp.bfloat16):
    drawn = scale * jax.random.normal(stream_key, dims, jnp.float32)
    if pieces:
        drawn = drawn * level_of(stream_key, dims, pieces, -0.22, 0.18)
    return jnp.clip(drawn, -bound, bound).astype(held_as)


def setup_inputs(seed: int = 0) -> dict:
    arg_keys = jax.random.split(jax.random.key(seed), 6)
    grid_input = normal_values(arg_keys[0], (LAT, LON * C), 1.0, 6.0, ((0, 8), (1, 4)))
    cotangent = normal_values(arg_keys[1], (LAT, C, LON), 1.0, 6.0, ((0, 8), (1, 4)))
    forward_legendre = normal_values(arg_keys[2], (LAT, ORDERS, DEGREES), LAT ** -0.5, 0.21875, ((1, 8),))
    inverse_legendre = normal_values(arg_keys[3], (LAT, ORDERS, DEGREES), DEGREES ** -0.5, 0.375, ((1, 8),))
    filter_weight = normal_values(arg_keys[4], (DEGREES, 2 * C * C), (2 * C) ** -0.5, 0.3125, ((0, 8),))
    return {"grid_input": grid_input, "cotangent": cotangent, "forward_legendre": forward_legendre, "inverse_legendre": inverse_legendre, "filter_weight": filter_weight}


def make_tables():
    longitude = jnp.arange(LON, dtype=jnp.int32)
    order_index = jnp.arange(ORDERS, dtype=jnp.int32)
    phases = (longitude[:, None] * order_index[None, :] % LON).astype(jnp.float32)
    angles = phases * (2.0 * math.pi / LON)
    factor = 1.0 / math.sqrt(LON)
    stacked = jnp.stack([jnp.cos(angles) * factor, -jnp.sin(angles) * factor], axis=-1)
    doubling = jnp.where(order_index == 0, 1.0, 2.0).astype(jnp.float32)
    basis_plain = stacked.reshape(LON, 2 * ORDERS).astype(jnp.bfloat16)
    basis_doubled = (stacked * doubling[None, :, None]).reshape(LON, 2 * ORDERS).astype(jnp.bfloat16)
    return (basis_plain, basis_doubled)

def degree_sum(field, matrix):
    row_count = LAT // N_POLAR
    running = jnp.zeros((DEGREES, ORDERS, 2, C), jnp.float32)
    for block in range(N_POLAR):
        field_part = field[block * row_count:(block + 1) * row_count].astype(jnp.float32)
        matrix_part = matrix[block * row_count:(block + 1) * row_count].astype(jnp.float32)
        partial_sum = jnp.einsum('amrc,aml->lmrc', field_part, matrix_part)
        rounded = lax.optimization_barrier(partial_sum.astype(jnp.bfloat16))
        running = running + rounded.astype(jnp.float32)
    return running.astype(jnp.bfloat16)

def degree_rows(modes, matrix):
    return jnp.einsum('lmrc,aml->amrc', modes.astype(jnp.float32), matrix.astype(jnp.float32)).astype(jnp.bfloat16)

def reference(grid_input, cotangent, forward_legendre, inverse_legendre, filter_weight):
    basis_plain, basis_doubled = make_tables()
    plain_wide = basis_plain.astype(jnp.float32)
    doubled_wide = basis_doubled.astype(jnp.float32)
    grid_cube = grid_input.reshape(LAT, LON, C)
    spectrum = jnp.einsum('alc,lj->ajc', grid_cube.astype(jnp.float32), plain_wide)
    spectrum = spectrum.astype(jnp.bfloat16).reshape(LAT, ORDERS, 2, C)
    coefficients = degree_sum(spectrum, forward_legendre).astype(jnp.float32)
    weight_cube = filter_weight.reshape(DEGREES, 2, C, C)
    weight_real = weight_cube[:, 0].astype(jnp.float32)
    weight_imag = weight_cube[:, 1].astype(jnp.float32)
    mixed_real = jnp.einsum('lmc,lco->lmo', coefficients[:, :, 0], weight_real) - jnp.einsum('lmc,lco->lmo', coefficients[:, :, 1], weight_imag)
    mixed_imag = jnp.einsum('lmc,lco->lmo', coefficients[:, :, 0], weight_imag) + jnp.einsum('lmc,lco->lmo', coefficients[:, :, 1], weight_real)
    mixed_modes = jnp.stack([mixed_real, mixed_imag], axis=2).astype(jnp.bfloat16)
    synthesis = degree_rows(mixed_modes, inverse_legendre)
    filtered = jnp.einsum('ajc,lj->acl', synthesis.reshape(LAT, 2 * ORDERS, C).astype(jnp.float32), doubled_wide).astype(jnp.bfloat16)
    grad_synthesis = jnp.einsum('acl,lj->ajc', cotangent.astype(jnp.float32), doubled_wide)
    grad_synthesis = grad_synthesis.astype(jnp.bfloat16).reshape(LAT, ORDERS, 2, C)
    grad_mixed = degree_sum(grad_synthesis, inverse_legendre).astype(jnp.float32)
    grad_real = jnp.einsum('lmo,lco->lmc', grad_mixed[:, :, 0], weight_real) + jnp.einsum('lmo,lco->lmc', grad_mixed[:, :, 1], weight_imag)
    grad_imag = jnp.einsum('lmo,lco->lmc', grad_mixed[:, :, 1], weight_real) - jnp.einsum('lmo,lco->lmc', grad_mixed[:, :, 0], weight_imag)
    grad_coefficients = jnp.stack([grad_real, grad_imag], axis=2).astype(jnp.bfloat16)
    grad_spectrum = degree_rows(grad_coefficients, forward_legendre)
    grid_grad = jnp.einsum('ajc,lj->alc', grad_spectrum.reshape(LAT, 2 * ORDERS, C).astype(jnp.float32), plain_wide).astype(jnp.bfloat16)
    return (filtered, grid_grad.reshape(LAT, LON * C))
```

```python
import math

import jax
import jax.numpy as jnp
import numpy as np
from jax import lax
from jax.experimental import pallas as pl
from jax.experimental.pallas import tpu as pltpu
from jax.sharding import PartitionSpec as P

LON = 1440
C = 192
ORDERS = 256
VMEM_BYTES = 48 * 1024 * 1024


def host_table():
    longitude = np.arange(LON)
    order = np.arange(ORDERS)
    angles = (order[:, None] * longitude[None, :] % LON) * (2.0 * math.pi / LON)
    stacked = np.concatenate([np.cos(angles), -np.sin(angles)], axis=0) / math.sqrt(LON)
    return jnp.asarray(stacked.astype(np.float32)).astype(jnp.bfloat16)


def double_orders(table):
    order = np.arange(2 * ORDERS) % ORDERS
    factor = np.where(order == 0, 1.0, 2.0).astype(np.float32)
    return (table.astype(jnp.float32) * factor[:, None]).astype(jnp.bfloat16)


def dot32(expression, left, right):
    return jnp.einsum(expression, left, right, preferred_element_type=jnp.float32).astype(jnp.bfloat16)


def rows_per_step(rows, most):
    return max(d for d in range(1, most + 1) if rows % d == 0)


def dot_f32(left, right, contract):
    return lax.dot_general(left, right, (contract, ((), ())), preferred_element_type=jnp.float32)


def store_orders(out_ref, row, value):
    polar, _, mine, _ = out_ref.shape
    for p in range(polar):
        out_ref[p, row] = value[p * mine:(p + 1) * mine]


def load_orders(in_ref, row):
    polar, _, mine, width = in_ref.shape
    return in_ref[:, row].reshape(polar * mine, width)


def call_rows(body, inputs, row_axes, out_shape, out_axis, step, flops):
    def block(shape, axis):
        if axis is None:
            return pl.BlockSpec(shape, lambda i: (0,) * len(shape))
        sizes = tuple(step if d == axis else s for d, s in enumerate(shape))
        return pl.BlockSpec(sizes, lambda i: tuple(i if d == axis else 0 for d in range(len(shape))))

    moved = sum(2 * math.prod(x.shape) for x in inputs) + 2 * math.prod(out_shape)
    return pl.pallas_call(
        body,
        grid=(out_shape[out_axis] // step,),
        in_specs=[block(x.shape, axis) for x, axis in zip(inputs, row_axes)],
        out_specs=block(out_shape, out_axis),
        out_shape=jax.ShapeDtypeStruct(out_shape, jnp.bfloat16),
        compiler_params=pltpu.CompilerParams(vmem_limit_bytes=VMEM_BYTES),
        cost_estimate=pl.CostEstimate(flops=flops, bytes_accessed=moved, transcendentals=0),
    )(*inputs)


def field_to_orders(cube, table, polar):
    lat, lon, chan = cube.shape

    def body(x_ref, table_ref, out_ref):
        def one(i, carry):
            y = dot_f32(table_ref[...], x_ref[i], ((1,), (0,)))
            both = jnp.concatenate([y[:ORDERS], y[ORDERS:]], axis=1)
            store_orders(out_ref, i, both.astype(jnp.bfloat16))
            return carry

        lax.fori_loop(0, x_ref.shape[0], one, 0)

    shape = (polar, lat, ORDERS // polar, 2 * chan)
    return call_rows(body, (cube, table), (0, None), shape, 1, rows_per_step(lat, 10),
                     4 * lat * lon * chan * ORDERS)


def orders_to_field(orders, table):
    polar, lat, mine, width = orders.shape
    lon, chan = table.shape[0], width // 2

    def body(g_ref, table_ref, out_ref):
        def one(i, carry):
            g = load_orders(g_ref, i)
            y = dot_f32(table_ref[:, :ORDERS], g[:, :chan], ((1,), (0,)))
            y += dot_f32(table_ref[:, ORDERS:], g[:, chan:], ((1,), (0,)))
            out_ref[i] = y.astype(jnp.bfloat16)
            return carry

        lax.fori_loop(0, out_ref.shape[0], one, 0)

    return call_rows(body, (orders, table), (1, None), (lat, lon, chan), 0, rows_per_step(lat, 10),
                     4 * lat * lon * chan * ORDERS)


def channels_to_orders(field, table, polar):
    lat, chan, lon = field.shape

    def body(x_ref, table_ref, out_ref):
        rows = x_ref.shape[0]
        x = x_ref[...].reshape(rows * chan, lon)
        y = dot_f32(table_ref[...], x, ((1,), (1,)))
        for i in range(rows):
            part = y[:, i * chan:(i + 1) * chan]
            both = jnp.concatenate([part[:ORDERS], part[ORDERS:]], axis=1)
            store_orders(out_ref, i, both.astype(jnp.bfloat16))

    shape = (polar, lat, ORDERS // polar, 2 * chan)
    return call_rows(body, (field, table), (0, None), shape, 1, rows_per_step(lat, 5),
                     4 * lat * lon * chan * ORDERS)


def orders_to_channels(orders, table):
    polar, lat, mine, width = orders.shape
    lon, chan = table.shape[1], width // 2

    def body(g_ref, table_ref, out_ref):
        rows = out_ref.shape[0]
        parts = [load_orders(g_ref, i).astype(jnp.float32) for i in range(rows)]
        real = jnp.concatenate([g[:, :chan] for g in parts], axis=1)
        imag = jnp.concatenate([g[:, chan:] for g in parts], axis=1)
        both = jnp.concatenate([real, imag], axis=0).astype(jnp.bfloat16)
        y = dot_f32(both, table_ref[...], ((0,), (0,)))
        out_ref[...] = y.astype(jnp.bfloat16).reshape(rows, chan, lon)

    return call_rows(body, (orders, table), (1, None), (lat, chan, lon), 0, rows_per_step(lat, 5),
                     4 * lat * lon * chan * ORDERS)


def exchange(blocks, axis):
    return lax.all_to_all(blocks, axis, split_axis=0, concat_axis=0, tiled=True)


def on_device(grid_input, cotangent, forward_legendre, inverse_legendre, filter_weight):
    azimuth = lax.axis_size("azimuth")
    polar = lax.axis_size("polar")
    plain = host_table()
    doubled = double_orders(plain)
    lat = grid_input.shape[0]
    lon = grid_input.shape[1] // C
    chan = cotangent.shape[1]
    total_lat, orders, degrees = forward_legendre.shape
    mine = orders // azimuth
    depth = degrees // polar
    local = lax.dynamic_slice_in_dim(plain, lax.axis_index("azimuth") * lon, lon, 1)

    spectrum = exchange(field_to_orders(grid_input.reshape(lat, lon, C), local, polar), "polar")
    grad_synthesis = exchange(channels_to_orders(cotangent, doubled, polar), "polar")

    weight = filter_weight.reshape(depth, 2, C, C)
    upper = jnp.concatenate([weight[:, 0], weight[:, 1]], axis=2)
    lower = jnp.concatenate([-weight[:, 1], weight[:, 0]], axis=2)
    kernel = jnp.concatenate([upper, lower], axis=1)

    grad_mixed = dot32(
        "amk,aml->mkl", grad_synthesis.reshape(total_lat, orders, 2 * chan), inverse_legendre
    )
    grad_mixed = exchange(grad_mixed, "azimuth").reshape(azimuth, mine, 2, chan, degrees)
    grad_mixed = grad_mixed.transpose(4, 1, 2, 0, 3).reshape(degrees, mine, 2 * C)
    grad_mixed = exchange(grad_mixed, "polar").reshape(polar, depth, mine, 2 * C)
    grad_modes = dot32("slmj,lkj->slmk", grad_mixed, kernel)
    grad_modes = exchange(grad_modes, "polar").reshape(degrees, mine, 2 * C)
    grad_modes = lax.all_gather(grad_modes.transpose(1, 0, 2), "azimuth", axis=0, tiled=True)

    coefficients = dot32(
        "amk,aml->mkl", spectrum.reshape(total_lat, orders, 2 * C), forward_legendre
    )
    coefficients = lax.psum_scatter(coefficients, "azimuth", scatter_dimension=0, tiled=True)
    coefficients = exchange(coefficients.transpose(2, 0, 1), "polar")
    mixed = dot32("slmk,lkj->slmj", coefficients.reshape(polar, depth, mine, 2 * C), kernel)
    mixed = exchange(mixed, "polar").reshape(degrees, mine, 2, azimuth, chan)
    mixed = mixed.transpose(3, 1, 0, 2, 4).reshape(orders, degrees, 2 * chan)
    mixed = exchange(mixed, "azimuth")

    grad_rows = dot32("mlk,aml->amk", grad_modes, forward_legendre)
    grad_rows = exchange(grad_rows.reshape(polar, lat, orders, 2 * C), "polar")
    rows = dot32("mlk,aml->amk", mixed, inverse_legendre)
    rows = exchange(rows.reshape(polar, lat, orders, 2 * chan), "polar")
    filtered = orders_to_channels(rows, doubled)
    grid_grad = orders_to_field(grad_rows, local.T)
    return filtered, grid_grad.reshape(lat, lon * C)


def solution(mesh):
    return jax.shard_map(
        on_device,
        mesh=mesh,
        in_specs=(
            P("polar", "azimuth"),
            P("polar", "azimuth", None),
            P(None, "polar", None),
            P(None, "polar", None),
            P("polar", None),
        ),
        out_specs=(P("polar", "azimuth", None), P("polar", "azimuth")),
        check_vma=False,
    )
```

```python
import math

import jax
import jax.numpy as jnp
import numpy as np
from jax import lax
from jax.experimental import pallas as pl
from jax.experimental.pallas import tpu as pltpu
from jax.sharding import PartitionSpec as P

LON = 1440
C = 192
ORDERS = 256
VMEM_BYTES = 48 * 1024 * 1024


def host_table():
    longitude = np.arange(LON)
    order = np.arange(ORDERS)
    angles = (order[:, None] * longitude[None, :] % LON) * (2.0 * math.pi / LON)
    stacked = np.concatenate([np.cos(angles), -np.sin(angles)], axis=0) / math.sqrt(LON)
    return jnp.asarray(stacked.astype(np.float32)).astype(jnp.bfloat16)


def double_orders(table):
    order = np.arange(2 * ORDERS) % ORDERS
    factor = np.where(order == 0, 1.0, 2.0).astype(np.float32)
    return (table.astype(jnp.float32) * factor[:, None]).astype(jnp.bfloat16)


def dot32(expression, left, right):
    return jnp.einsum(expression, left, right, preferred_element_type=jnp.float32).astype(jnp.bfloat16)


def rows_per_step(rows, most):
    return max(d for d in range(1, most + 1) if rows % d == 0)


def dot_f32(left, right, contract):
    return lax.dot_general(left, right, (contract, ((), ())), preferred_element_type=jnp.float32)


def store_orders(out_ref, row, value):
    polar, _, mine, _ = out_ref.shape
    for p in range(polar):
        out_ref[p, row] = value[p * mine:(p + 1) * mine]


def load_orders(in_ref, row):
    polar, _, mine, width = in_ref.shape
    return in_ref[:, row].reshape(polar * mine, width)


def call_rows(body, inputs, row_axes, out_shape, out_axis, step, flops):
    def block(shape, axis):
        if axis is None:
            return pl.BlockSpec(shape, lambda i: (0,) * len(shape))
        sizes = tuple(step if d == axis else s for d, s in enumerate(shape))
        return pl.BlockSpec(sizes, lambda i: tuple(i if d == axis else 0 for d in range(len(shape))))

    moved = sum(2 * math.prod(x.shape) for x in inputs) + 2 * math.prod(out_shape)
    return pl.pallas_call(
        body,
        grid=(out_shape[out_axis] // step,),
        in_specs=[block(x.shape, axis) for x, axis in zip(inputs, row_axes)],
        out_specs=block(out_shape, out_axis),
        out_shape=jax.ShapeDtypeStruct(out_shape, jnp.bfloat16),
        compiler_params=pltpu.CompilerParams(vmem_limit_bytes=VMEM_BYTES),
        cost_estimate=pl.CostEstimate(flops=flops, bytes_accessed=moved, transcendentals=0),
    )(*inputs)


def field_to_orders(cube, table, polar):
    lat, lon, chan = cube.shape

    def body(x_ref, table_ref, out_ref):
        def one(i, carry):
            y = dot_f32(table_ref[...], x_ref[i], ((1,), (0,)))
            both = jnp.concatenate([y[:ORDERS], y[ORDERS:]], axis=1)
            store_orders(out_ref, i, both.astype(jnp.bfloat16))
            return carry

        lax.fori_loop(0, x_ref.shape[0], one, 0)

    shape = (polar, lat, ORDERS // polar, 2 * chan)
    return call_rows(body, (cube, table), (0, None), shape, 1, rows_per_step(lat, 10),
                     4 * lat * lon * chan * ORDERS)


def orders_to_field(orders, table):
    polar, lat, mine, width = orders.shape
    lon, chan = table.shape[0], width // 2

    def body(g_ref, table_ref, out_ref):
        def one(i, carry):
            g = load_orders(g_ref, i)
            y = dot_f32(table_ref[:, :ORDERS], g[:, :chan], ((1,), (0,)))
            y += dot_f32(table_ref[:, ORDERS:], g[:, chan:], ((1,), (0,)))
            out_ref[i] = y.astype(jnp.bfloat16)
            return carry

        lax.fori_loop(0, out_ref.shape[0], one, 0)

    return call_rows(body, (orders, table), (1, None), (lat, lon, chan), 0, rows_per_step(lat, 10),
                     4 * lat * lon * chan * ORDERS)


def channels_to_orders(field, table, polar):
    lat, chan, lon = field.shape

    def body(x_ref, table_ref, out_ref):
        rows = x_ref.shape[0]
        x = x_ref[...].reshape(rows * chan, lon)
        y = dot_f32(table_ref[...], x, ((1,), (1,)))
        for i in range(rows):
            part = y[:, i * chan:(i + 1) * chan]
            both = jnp.concatenate([part[:ORDERS], part[ORDERS:]], axis=1)
            store_orders(out_ref, i, both.astype(jnp.bfloat16))

    shape = (polar, lat, ORDERS // polar, 2 * chan)
    return call_rows(body, (field, table), (0, None), shape, 1, rows_per_step(lat, 5),
                     4 * lat * lon * chan * ORDERS)


def orders_to_channels(orders, table):
    polar, lat, mine, width = orders.shape
    lon, chan = table.shape[1], width // 2

    def body(g_ref, table_ref, out_ref):
        rows = out_ref.shape[0]
        parts = [load_orders(g_ref, i).astype(jnp.float32) for i in range(rows)]
        real = jnp.concatenate([g[:, :chan] for g in parts], axis=1)
        imag = jnp.concatenate([g[:, chan:] for g in parts], axis=1)
        both = jnp.concatenate([real, imag], axis=0).astype(jnp.bfloat16)
        y = dot_f32(both, table_ref[...], ((0,), (0,)))
        out_ref[...] = y.astype(jnp.bfloat16).reshape(rows, chan, lon)

    return call_rows(body, (orders, table), (1, None), (lat, chan, lon), 0, rows_per_step(lat, 5),
                     4 * lat * lon * chan * ORDERS)


def lane_tiles(width):
    return -(-width // 128)


def split_rows(in_ref, wide_ref):
    rows, block, width = in_ref.shape
    for j in range(lane_tiles(width)):
        lanes = min(128, width - 128 * j)
        part = in_ref[:, :, 128 * j:128 * j + lanes].astype(jnp.float32)
        wide_ref[j, :rows * block, :lanes] = part.reshape(rows * block, lanes)


def order_rows(wide_ref, m, rows, block):
    parts = [wide_ref[j, pl.ds(m, rows, stride=block), :] for j in range(wide_ref.shape[0])]
    return jnp.concatenate(parts, axis=1).astype(jnp.bfloat16)


def legendre_blocks(table):
    rows, orders, _ = table.shape
    block = 16 if orders % 16 == 0 else orders
    step = max(d for d in range(8, 241, 8) if rows % d == 0)
    return step, block


def analysis(field, table, degrees_first):
    rows, orders, width = field.shape
    degrees = table.shape[2]
    step, block = legendre_blocks(table)
    shape = (degrees, width) if degrees_first else (width, degrees)

    def body(s_ref, f_ref, out_ref, s_wide, f_wide, total):
        split_rows(s_ref, s_wide)
        split_rows(f_ref, f_wide)

        @pl.when(pl.program_id(1) == 0)
        def _():
            total[...] = jnp.zeros_like(total)

        for m in range(block):
            s = order_rows(s_wide, m, step, block)[:, :width]
            f = order_rows(f_wide, m, step, block)
            pair = (f, s) if degrees_first else (s, f)
            total[m] += dot_f32(*pair, ((0,), (0,)))

        @pl.when(pl.program_id(1) == pl.num_programs(1) - 1)
        def _():
            out_ref[...] = total[...].astype(jnp.bfloat16)

    return pl.pallas_call(
        body,
        grid=(orders // block, rows // step),
        in_specs=[
            pl.BlockSpec((step, block, width), lambda i, j: (j, i, 0)),
            pl.BlockSpec((step, block, degrees), lambda i, j: (j, i, 0)),
        ],
        out_specs=pl.BlockSpec((block, *shape), lambda i, j: (i, 0, 0)),
        out_shape=jax.ShapeDtypeStruct((orders, *shape), jnp.bfloat16),
        scratch_shapes=[
            pltpu.VMEM((lane_tiles(width), (step + 1) * block, 128), jnp.float32),
            pltpu.VMEM((lane_tiles(degrees), (step + 1) * block, 128), jnp.float32),
            pltpu.VMEM((block, *shape), jnp.float32),
        ],
        compiler_params=pltpu.CompilerParams(vmem_limit_bytes=VMEM_BYTES),
        cost_estimate=pl.CostEstimate(
            flops=2 * rows * orders * width * degrees,
            bytes_accessed=2 * rows * orders * (width + degrees),
            transcendentals=0,
        ),
    )(field, table)


def synthesis(modes, table):
    orders, degrees, width = modes.shape
    rows = table.shape[0]
    step, block = legendre_blocks(table)
    tiles = lane_tiles(width)

    def body(g_ref, f_ref, out_ref, f_wide, out_wide):
        split_rows(f_ref, f_wide)
        for m in range(block):
            f = order_rows(f_wide, m, step, block)
            y = dot_f32(f, g_ref[m], ((1,), (0,)))
            if width % 128:
                fill = jnp.zeros((step, 128 * tiles - width), jnp.float32)
                y = jnp.concatenate([y, fill], axis=1)
            for j in range(tiles):
                out_wide[j, pl.ds(m, step, stride=block), :] = y[:, 128 * j:128 * (j + 1)]
        for j in range(tiles):
            lanes = min(128, width - 128 * j)
            part = out_wide[j, :step * block].reshape(step, block, 128)[:, :, :lanes]
            out_ref[:, :, 128 * j:128 * j + lanes] = part.astype(jnp.bfloat16)

    return pl.pallas_call(
        body,
        grid=(orders // block, rows // step),
        in_specs=[
            pl.BlockSpec((block, degrees, width), lambda i, j: (i, 0, 0)),
            pl.BlockSpec((step, block, degrees), lambda i, j: (j, i, 0)),
        ],
        out_specs=pl.BlockSpec((step, block, width), lambda i, j: (j, i, 0)),
        out_shape=jax.ShapeDtypeStruct((rows, orders, width), jnp.bfloat16),
        scratch_shapes=[
            pltpu.VMEM((lane_tiles(degrees), (step + 1) * block, 128), jnp.float32),
            pltpu.VMEM((tiles, (step + 1) * block, 128), jnp.float32),
        ],
        compiler_params=pltpu.CompilerParams(vmem_limit_bytes=VMEM_BYTES),
        cost_estimate=pl.CostEstimate(
            flops=2 * rows * orders * width * degrees,
            bytes_accessed=2 * rows * orders * (width + degrees),
            transcendentals=0,
        ),
    )(modes, table)


def exchange(blocks, axis):
    return lax.all_to_all(blocks, axis, split_axis=0, concat_axis=0, tiled=True)


def on_device(grid_input, cotangent, forward_legendre, inverse_legendre, filter_weight):
    azimuth = lax.axis_size("azimuth")
    polar = lax.axis_size("polar")
    plain = host_table()
    doubled = double_orders(plain)
    lat = grid_input.shape[0]
    lon = grid_input.shape[1] // C
    chan = cotangent.shape[1]
    total_lat, orders, degrees = forward_legendre.shape
    mine = orders // azimuth
    depth = degrees // polar
    local = lax.dynamic_slice_in_dim(plain, lax.axis_index("azimuth") * lon, lon, 1)

    grad_synthesis = exchange(channels_to_orders(cotangent, doubled, polar), "polar")
    spectrum = field_to_orders(grid_input.reshape(lat, lon, C), local, polar)

    grad_synthesis, spectrum = lax.optimization_barrier((grad_synthesis, spectrum))

    weight = filter_weight.reshape(depth, 2, C, C)
    upper = jnp.concatenate([weight[:, 0], weight[:, 1]], axis=2)
    lower = jnp.concatenate([-weight[:, 1], weight[:, 0]], axis=2)
    kernel = jnp.concatenate([upper, lower], axis=1)

    grad_mixed = analysis(
        grad_synthesis.reshape(total_lat, orders, 2 * chan), inverse_legendre, False
    )
    grad_mixed = exchange(grad_mixed, "azimuth").reshape(azimuth, mine, 2, chan, degrees)
    grad_mixed = grad_mixed.transpose(4, 1, 2, 0, 3).reshape(degrees, mine, 2 * C)
    grad_mixed = exchange(grad_mixed, "polar").reshape(polar, depth, mine, 2 * C)
    grad_modes = dot32("slmj,lkj->slmk", grad_mixed, kernel)
    grad_modes = exchange(grad_modes, "polar").reshape(degrees, mine, 2 * C)
    grad_modes, spectrum = lax.optimization_barrier((grad_modes.transpose(1, 0, 2), spectrum))
    grad_modes = lax.all_gather(grad_modes, "azimuth", axis=0, tiled=True)

    spectrum = exchange(spectrum, "polar").reshape(total_lat, orders, 2 * C)
    coefficients = analysis(spectrum, forward_legendre, True)
    coefficients, grad_modes = lax.optimization_barrier((coefficients, grad_modes))
    coefficients = lax.psum_scatter(coefficients, "azimuth", scatter_dimension=0, tiled=True)
    grad_rows = synthesis(grad_modes, forward_legendre)
    grad_rows = exchange(grad_rows.reshape(polar, lat, orders, 2 * C), "polar")

    coefficients = exchange(coefficients.transpose(1, 0, 2), "polar")
    mixed = dot32("slmk,lkj->slmj", coefficients.reshape(polar, depth, mine, 2 * C), kernel)
    mixed = exchange(mixed, "polar").reshape(degrees, mine, 2, azimuth, chan)
    mixed = mixed.transpose(3, 1, 0, 2, 4).reshape(orders, degrees, 2 * chan)
    rows = synthesis(exchange(mixed, "azimuth"), inverse_legendre)
    rows = exchange(rows.reshape(polar, lat, orders, 2 * chan), "polar")
    filtered = orders_to_channels(rows, doubled)
    grid_grad = orders_to_field(grad_rows, local.T)
    return filtered, grid_grad.reshape(lat, lon * C)


def solution(mesh):
    return jax.shard_map(
        on_device,
        mesh=mesh,
        in_specs=(
            P("polar", "azimuth"),
            P("polar", "azimuth", None),
            P(None, "polar", None),
            P(None, "polar", None),
            P("polar", None),
        ),
        out_specs=(P("polar", "azimuth", None), P("polar", "azimuth")),
        check_vma=False,
    )
```

```python
import math

import jax
import jax.numpy as jnp
import numpy as np
from jax import lax
from jax.experimental import pallas as pl
from jax.experimental.pallas import tpu as pltpu
from jax.sharding import PartitionSpec as P

LON = 1440
C = 192
ORDERS = 256
VMEM_BYTES = 48 * 1024 * 1024


def host_table():
    longitude = np.arange(LON)
    order = np.arange(ORDERS)
    angles = (order[:, None] * longitude[None, :] % LON) * (2.0 * math.pi / LON)
    stacked = np.concatenate([np.cos(angles), -np.sin(angles)], axis=0) / math.sqrt(LON)
    return jnp.asarray(stacked.astype(np.float32)).astype(jnp.bfloat16)


def double_orders(table):
    order = np.arange(2 * ORDERS) % ORDERS
    factor = np.where(order == 0, 1.0, 2.0).astype(np.float32)
    return (table.astype(jnp.float32) * factor[:, None]).astype(jnp.bfloat16)


def dot32(expression, left, right):
    return jnp.einsum(expression, left, right, preferred_element_type=jnp.float32).astype(jnp.bfloat16)


def rows_per_step(rows, most):
    return max(d for d in range(1, most + 1) if rows % d == 0)


def dot_f32(left, right, contract):
    return lax.dot_general(left, right, (contract, ((), ())), preferred_element_type=jnp.float32)


def store_orders(out_ref, row, value):
    polar, _, mine, _ = out_ref.shape
    for p in range(polar):
        out_ref[p, row] = value[p * mine:(p + 1) * mine]


def load_orders(in_ref, row):
    polar, _, mine, width = in_ref.shape
    return in_ref[:, row].reshape(polar * mine, width)


def call_rows(body, inputs, row_axes, out_shape, out_axis, step, flops):
    def block(shape, axis):
        if axis is None:
            return pl.BlockSpec(shape, lambda i: (0,) * len(shape))
        sizes = tuple(step if d == axis else s for d, s in enumerate(shape))
        return pl.BlockSpec(sizes, lambda i: tuple(i if d == axis else 0 for d in range(len(shape))))

    moved = sum(2 * math.prod(x.shape) for x in inputs) + 2 * math.prod(out_shape)
    return pl.pallas_call(
        body,
        grid=(out_shape[out_axis] // step,),
        in_specs=[block(x.shape, axis) for x, axis in zip(inputs, row_axes)],
        out_specs=block(out_shape, out_axis),
        out_shape=jax.ShapeDtypeStruct(out_shape, jnp.bfloat16),
        compiler_params=pltpu.CompilerParams(vmem_limit_bytes=VMEM_BYTES),
        cost_estimate=pl.CostEstimate(flops=flops, bytes_accessed=moved, transcendentals=0),
    )(*inputs)


def field_to_orders(cube, table, polar):
    lat, lon, chan = cube.shape

    def body(x_ref, table_ref, out_ref):
        def one(i, carry):
            y = dot_f32(table_ref[...], x_ref[i], ((1,), (0,)))
            both = jnp.concatenate([y[:ORDERS], y[ORDERS:]], axis=1)
            store_orders(out_ref, i, both.astype(jnp.bfloat16))
            return carry

        lax.fori_loop(0, x_ref.shape[0], one, 0)

    shape = (polar, lat, ORDERS // polar, 2 * chan)
    return call_rows(body, (cube, table), (0, None), shape, 1, rows_per_step(lat, 10),
                     4 * lat * lon * chan * ORDERS)


def orders_to_field(orders, table):
    polar, lat, mine, width = orders.shape
    lon, chan = table.shape[0], width // 2

    def body(g_ref, table_ref, out_ref):
        def one(i, carry):
            g = load_orders(g_ref, i)
            y = dot_f32(table_ref[:, :ORDERS], g[:, :chan], ((1,), (0,)))
            y += dot_f32(table_ref[:, ORDERS:], g[:, chan:], ((1,), (0,)))
            out_ref[i] = y.astype(jnp.bfloat16)
            return carry

        lax.fori_loop(0, out_ref.shape[0], one, 0)

    return call_rows(body, (orders, table), (1, None), (lat, lon, chan), 0, rows_per_step(lat, 10),
                     4 * lat * lon * chan * ORDERS)


def channels_to_orders(field, table, polar):
    lat, chan, lon = field.shape

    def body(x_ref, table_ref, out_ref):
        rows = x_ref.shape[0]
        x = x_ref[...].reshape(rows * chan, lon)
        y = dot_f32(table_ref[...], x, ((1,), (1,)))
        for i in range(rows):
            part = y[:, i * chan:(i + 1) * chan]
            both = jnp.concatenate([part[:ORDERS], part[ORDERS:]], axis=1)
            store_orders(out_ref, i, both.astype(jnp.bfloat16))

    shape = (polar, lat, ORDERS // polar, 2 * chan)
    return call_rows(body, (field, table), (0, None), shape, 1, rows_per_step(lat, 5),
                     4 * lat * lon * chan * ORDERS)


def orders_to_channels(orders, table):
    polar, lat, mine, width = orders.shape
    lon, chan = table.shape[1], width // 2

    def body(g_ref, table_ref, out_ref):
        rows = out_ref.shape[0]
        parts = [load_orders(g_ref, i).astype(jnp.float32) for i in range(rows)]
        real = jnp.concatenate([g[:, :chan] for g in parts], axis=1)
        imag = jnp.concatenate([g[:, chan:] for g in parts], axis=1)
        both = jnp.concatenate([real, imag], axis=0).astype(jnp.bfloat16)
        y = dot_f32(both, table_ref[...], ((0,), (0,)))
        out_ref[...] = y.astype(jnp.bfloat16).reshape(rows, chan, lon)

    return call_rows(body, (orders, table), (1, None), (lat, chan, lon), 0, rows_per_step(lat, 5),
                     4 * lat * lon * chan * ORDERS)


def lane_tiles(width):
    return -(-width // 128)


def split_rows(in_ref, wide_ref):
    rows, block, width = in_ref.shape
    for j in range(lane_tiles(width)):
        lanes = min(128, width - 128 * j)
        part = in_ref[:, :, 128 * j:128 * j + lanes].astype(jnp.float32)
        wide_ref[j, :rows * block, :lanes] = part.reshape(rows * block, lanes)


def order_rows(wide_ref, m, rows, block):
    parts = [wide_ref[j, pl.ds(m, rows, stride=block), :] for j in range(wide_ref.shape[0])]
    return jnp.concatenate(parts, axis=1).astype(jnp.bfloat16)


def legendre_blocks(table):
    rows, orders, _ = table.shape
    block = 16 if orders % 16 == 0 else orders
    step = max(d for d in range(8, 241, 8) if rows % d == 0)
    return step, block


def analysis(field, table, degrees_first):
    rows, orders, width = field.shape
    degrees = table.shape[2]
    step, block = legendre_blocks(table)
    shape = (degrees, width) if degrees_first else (width, degrees)

    def body(s_ref, f_ref, out_ref, s_wide, f_wide, total):
        split_rows(s_ref, s_wide)
        split_rows(f_ref, f_wide)

        @pl.when(pl.program_id(1) == 0)
        def _():
            total[...] = jnp.zeros_like(total)

        for m in range(block):
            s = order_rows(s_wide, m, step, block)[:, :width]
            f = order_rows(f_wide, m, step, block)
            pair = (f, s) if degrees_first else (s, f)
            total[m] += dot_f32(*pair, ((0,), (0,)))

        @pl.when(pl.program_id(1) == pl.num_programs(1) - 1)
        def _():
            out_ref[...] = total[...].astype(jnp.bfloat16)

    return pl.pallas_call(
        body,
        grid=(orders // block, rows // step),
        in_specs=[
            pl.BlockSpec((step, block, width), lambda i, j: (j, i, 0)),
            pl.BlockSpec((step, block, degrees), lambda i, j: (j, i, 0)),
        ],
        out_specs=pl.BlockSpec((block, *shape), lambda i, j: (i, 0, 0)),
        out_shape=jax.ShapeDtypeStruct((orders, *shape), jnp.bfloat16),
        scratch_shapes=[
            pltpu.VMEM((lane_tiles(width), (step + 1) * block, 128), jnp.float32),
            pltpu.VMEM((lane_tiles(degrees), (step + 1) * block, 128), jnp.float32),
            pltpu.VMEM((block, *shape), jnp.float32),
        ],
        compiler_params=pltpu.CompilerParams(vmem_limit_bytes=VMEM_BYTES),
        cost_estimate=pl.CostEstimate(
            flops=2 * rows * orders * width * degrees,
            bytes_accessed=2 * rows * orders * (width + degrees),
            transcendentals=0,
        ),
    )(field, table)


def synthesis(modes, table):
    orders, degrees, width = modes.shape
    rows = table.shape[0]
    step, block = legendre_blocks(table)
    tiles = lane_tiles(width)

    def body(g_ref, f_ref, out_ref, f_wide, out_wide):
        split_rows(f_ref, f_wide)
        for m in range(block):
            f = order_rows(f_wide, m, step, block)
            y = dot_f32(f, g_ref[m], ((1,), (0,)))
            if width % 128:
                fill = jnp.zeros((step, 128 * tiles - width), jnp.float32)
                y = jnp.concatenate([y, fill], axis=1)
            for j in range(tiles):
                out_wide[j, pl.ds(m, step, stride=block), :] = y[:, 128 * j:128 * (j + 1)]
        for j in range(tiles):
            lanes = min(128, width - 128 * j)
            part = out_wide[j, :step * block].reshape(step, block, 128)[:, :, :lanes]
            out_ref[:, :, 128 * j:128 * j + lanes] = part.astype(jnp.bfloat16)

    return pl.pallas_call(
        body,
        grid=(orders // block, rows // step),
        in_specs=[
            pl.BlockSpec((block, degrees, width), lambda i, j: (i, 0, 0)),
            pl.BlockSpec((step, block, degrees), lambda i, j: (j, i, 0)),
        ],
        out_specs=pl.BlockSpec((step, block, width), lambda i, j: (j, i, 0)),
        out_shape=jax.ShapeDtypeStruct((rows, orders, width), jnp.bfloat16),
        scratch_shapes=[
            pltpu.VMEM((lane_tiles(degrees), (step + 1) * block, 128), jnp.float32),
            pltpu.VMEM((tiles, (step + 1) * block, 128), jnp.float32),
        ],
        compiler_params=pltpu.CompilerParams(vmem_limit_bytes=VMEM_BYTES),
        cost_estimate=pl.CostEstimate(
            flops=2 * rows * orders * width * degrees,
            bytes_accessed=2 * rows * orders * (width + degrees),
            transcendentals=0,
        ),
    )(modes, table)


def exchange(blocks, axis):
    return lax.all_to_all(blocks, axis, split_axis=0, concat_axis=0, tiled=True)


def on_device(grid_input, cotangent, forward_legendre, inverse_legendre, filter_weight):
    azimuth = lax.axis_size("azimuth")
    polar = lax.axis_size("polar")
    plain = host_table()
    doubled = double_orders(plain)
    lat = grid_input.shape[0]
    lon = grid_input.shape[1] // C
    chan = cotangent.shape[1]
    total_lat, orders, degrees = forward_legendre.shape
    mine = orders // azimuth
    depth = degrees // polar
    local = lax.dynamic_slice_in_dim(plain, lax.axis_index("azimuth") * lon, lon, 1)

    grad_synthesis = exchange(channels_to_orders(cotangent, doubled, polar), "polar")
    spectrum = field_to_orders(grid_input.reshape(lat, lon, C), local, polar)

    grad_synthesis, spectrum = lax.optimization_barrier((grad_synthesis, spectrum))

    weight = filter_weight.reshape(depth, 2, C, C)
    upper = jnp.concatenate([weight[:, 0], weight[:, 1]], axis=2)
    lower = jnp.concatenate([-weight[:, 1], weight[:, 0]], axis=2)
    kernel = jnp.concatenate([upper, lower], axis=1)

    grad_mixed = analysis(
        grad_synthesis.reshape(total_lat, orders, 2 * chan), inverse_legendre, False
    )
    grad_mixed = exchange(grad_mixed, "azimuth").reshape(azimuth, mine, 2, chan, degrees)
    grad_mixed = grad_mixed.transpose(4, 1, 2, 0, 3).reshape(degrees, mine, 2 * C)
    grad_mixed = exchange(grad_mixed, "polar").reshape(polar, depth, mine, 2 * C)
    grad_modes = dot32("slmj,lkj->slmk", grad_mixed, kernel)
    grad_modes = exchange(grad_modes, "polar").reshape(degrees, mine, 2 * C)
    grad_modes, spectrum = lax.optimization_barrier((grad_modes.transpose(1, 0, 2), spectrum))
    grad_modes = lax.all_gather(grad_modes, "azimuth", axis=0, tiled=True)

    spectrum = exchange(spectrum, "polar").reshape(total_lat, orders, 2 * C)
    coefficients = analysis(spectrum, forward_legendre, True)
    coefficients, grad_modes = lax.optimization_barrier((coefficients, grad_modes))
    coefficients = lax.psum_scatter(coefficients, "azimuth", scatter_dimension=0, tiled=True)
    grad_rows = synthesis(grad_modes, forward_legendre)
    grad_rows = exchange(grad_rows.reshape(polar, lat, orders, 2 * C), "polar")
    coefficients, grad_rows = lax.optimization_barrier((coefficients, grad_rows))

    coefficients = exchange(coefficients.transpose(1, 0, 2), "polar")
    mixed = dot32("slmk,lkj->slmj", coefficients.reshape(polar, depth, mine, 2 * C), kernel)
    mixed = exchange(mixed, "polar").reshape(degrees, mine, 2, azimuth, chan)
    mixed = mixed.transpose(3, 1, 0, 2, 4).reshape(orders, degrees, 2 * chan)
    rows = synthesis(exchange(mixed, "azimuth"), inverse_legendre)
    rows = exchange(rows.reshape(polar, lat, orders, 2 * chan), "polar")
    filtered = orders_to_channels(rows, doubled)
    grid_grad = orders_to_field(grad_rows, local.T)
    return filtered, grid_grad.reshape(lat, lon * C)


def solution(mesh):
    return jax.shard_map(
        on_device,
        mesh=mesh,
        in_specs=(
            P("polar", "azimuth"),
            P("polar", "azimuth", None),
            P(None, "polar", None),
            P(None, "polar", None),
            P("polar", None),
        ),
        out_specs=(P("polar", "azimuth", None), P("polar", "azimuth")),
        check_vma=False,
    )
```
